32 devices in a mesh: ga: 2 (over x), col: 16 (over z, y, core).
Axes of the slice: x: 2, y: 2, z: 4, core: 2. Of those that a mesh axis runs over, the one named last changes fastest.
Arguments:
- cholesky: bfloat16 [1024, 1024, 512], P(('ga', 'col')), parts along dimension 0, may hold values from -0.1875 to 0.1875
- amplitudes: bfloat16 [512, 512, 512], P('ga', 'col'), parts along dimension 0, may hold values from -0.25 to 0.25
Outputs:
- ladder: float32 [512, 2, 512], P('ga', None, 'col'), parts along dimension 0
The draws below stay inside these ranges and needn't reach their ends.
There are 2 independent parts, one for each index of `ga`. The reference program is written for one: setup_inputs(seed, part) draws one part's arguments, and reference() takes and returns one part's arrays. A program takes and returns all parts, laid end to end along the dimension named above; each array names one. Nothing has to cross between parts.
All inputs are finite; a program needn't handle non-finite values.
Results may differ from the reference program's by a relative error of at most 0.0029.
Values may be sent and summed in bfloat16 or wider, within the bound.
A program may use at most 128 MiB of HBM per device.

```python
import jax
import jax.numpy as jnp
from jax import lax

V = 512
NCHOL = 1024
A_WIN = 2
P_SIZE = 256


def level_of(rng, dims, split, smallest, largest):
    def one(dim, parts):
        heights = jax.random.uniform(jax.random.fold_in(jax.random.fold_in(rng, 6), dim), (parts,), jnp.float32, smallest / len(split), largest / len(split))
        return jnp.repeat(jnp.exp(heights), dims[dim] // parts).reshape((-1,) + (1,) * (len(dims) - dim - 1))

    loudness = one(*split[0])
    for cut in split[1:]:
        loudness = loudness * one(*cut)
    return loudness


def centred(key, dims, spread, limit, shards=(), kind=jnp.bfloat16):
    drawn = spread * jax.random.normal(key, dims, jnp.float32)
    if shards:
        drawn = drawn * level_of(key, dims, shards, -0.22, 0.18)
    return jnp.clip(drawn, -limit, limit).astype(kind)


def setup_inputs(seed: int = 0, part: int = 0) -> dict:
    arg_keys = jax.random.split(jax.random.key(seed), 3)
    own_keys = jax.random.split(jax.random.fold_in(arg_keys[2], part), 3)
    return {
        "cholesky": centred(own_keys[0], (V, NCHOL, V), NCHOL ** -0.5, 0.1875, ((0, 16),)),
        "amplitudes": centred(own_keys[1], (P_SIZE, V, V), V ** -0.5, 0.25, ((1, 16),)),
    }


def reference(cholesky, amplitudes):
    window = cholesky[:, :, :A_WIN].astype(jnp.float32)
    block_rows = min(64, V)

    def advance(index, running):
        offset = (index * block_rows).astype(jnp.int32)
        chol_block = lax.dynamic_slice_in_dim(cholesky, offset, block_rows, 0).astype(jnp.float32)
        amp_block = lax.dynamic_slice_in_dim(amplitudes, offset, block_rows, 1).astype(jnp.float32)
        integrals = jnp.einsum("clb,dla->acbd", chol_block, window, precision=lax.Precision.HIGHEST)
        integrals = integrals.astype(jnp.bfloat16).astype(jnp.float32)
        return running + jnp.einsum("pcd,acbd->pab", amp_block, integrals, precision=lax.Precision.HIGHEST)

    initial = jnp.zeros((P_SIZE, A_WIN, V), jnp.float32)
    return lax.fori_loop(0, V // block_rows, advance, initial)
```

```python
import functools

import jax
import jax.numpy as jnp
from jax import lax
from jax.experimental import pallas as pl
from jax.experimental.pallas import tpu as pltpu
from jax.sharding import PartitionSpec as P

A_WIN = 2
PHASES = 2
F32 = jnp.float32
BF16 = jnp.bfloat16
MESH = pl.DeviceIdType.MESH


def kernel(n, lc, group, pc, chol, amps, out, bv, tt, traw, tf, sel, w, wa, xbuf, acc, acct,
           recv_a, summed, recv_b, lane_sem, rest_sem, t_sem, g_send, g_recv, f_send, f_recv,
           a_send, a_recv, b_send, b_recv):
    c_loc, nchol, v = chol.shape
    p_size = amps.shape[0]
    q_num = nchol // lc
    k_num = n // 2
    vb = v // n
    ph_rows = p_size // PHASES
    me = lax.axis_index("col")
    chip = me // 2
    core = lax.rem(me, 2)
    sib = chip * 2 + 1 - core

    def peer_at(i):
        return lax.rem(chip + i, k_num) * 2 + core

    def source_at(i):
        return lax.rem(chip - i + k_num, k_num) * 2 + core

    def lane_copy(q):
        rows = pl.ds(q * lc, lc)
        return pltpu.make_async_copy(chol.at[:, rows, pl.ds(0, 128)], bv.at[:, rows, pl.ds(0, 128)], lane_sem.at[q])

    def rest_copy(q):
        rows = pl.ds(q * lc, lc)
        return pltpu.make_async_copy(chol.at[:, rows, pl.ds(128, v - 128)], bv.at[:, rows, pl.ds(128, v - 128)], rest_sem.at[q])

    t_num = p_size // pc

    def t_copy(i):
        return pltpu.make_async_copy(amps.at[pl.ds(i * pc, pc)], traw.at[i % 2], t_sem.at[i % 2])

    for q in range(q_num):
        lane_copy(q).start()
    t_copy(0).start()
    t_copy(1).start()
    for q in range(q_num):
        rest_copy(q).start()

    barrier = pltpu.get_barrier_semaphore()
    pl.semaphore_signal(barrier, inc=1, device_id={"col": sib}, device_id_type=MESH)
    for i in range(1, k_num):
        pl.semaphore_signal(barrier, inc=1, device_id={"col": peer_at(i)}, device_id_type=MESH)

    lane = lax.broadcasted_iota(jnp.int32, (128, 128), 0)
    column = lax.broadcasted_iota(jnp.int32, (128, 128), 1)

    def make_sel(c, _):
        sel[c] = jnp.where((lane < A_WIN) & (column == lane * c_loc + c), 1.0, 0.0).astype(BF16)
        return 0

    lax.fori_loop(0, c_loc, make_sel, 0)
    pl.semaphore_wait(barrier, k_num)

    def remote(src, dst, send, recv, to):
        return pltpu.make_async_remote_copy(
            src_ref=src, dst_ref=dst, send_sem=send, recv_sem=recv, device_id={"col": to}, device_id_type=MESH)

    def gather_copy(q, i):
        to = sib if i == 0 else peer_at(i)
        return remote(w.at[q, me], w.at[q, me], g_send.at[q, i], g_recv.at[q, i], to)

    def forward_copy(q, i):
        block = w.at[q, source_at(i)]
        return remote(block, block, f_send.at[q, i], f_recv.at[q, i], sib)

    def extract(q):
        lane_copy(q).wait()

        def step(c, z):
            return z + jnp.dot(bv[c, pl.ds(q * lc, lc), pl.ds(0, 128)], sel[c], preferred_element_type=F32)

        z = lax.fori_loop(0, c_loc, step, jnp.zeros((lc, 128), F32), unroll=4)
        w[q, me] = jnp.transpose(z)[: A_WIN * c_loc].astype(BF16)
        for i in range(k_num):
            gather_copy(q, i).start()

    def forward(q):
        for i in range(1, k_num):
            gather_copy(q, i).wait_recv()
            forward_copy(q, i).start()

    def finish(q):
        gather_copy(q, 0).wait_recv()
        for i in range(1, k_num):
            forward_copy(q, i).wait_recv()
        whole = w[q].astype(F32)
        for a in range(A_WIN):
            wa[q, a] = whole[:, a * c_loc : (a + 1) * c_loc, :].reshape(v, lc).astype(BF16)

    def turn(i):
        t_copy(i).wait()
        for j in range(0, v, 128):
            tf[j // 128] = traw[i % 2, :, :, pl.ds(j, 128)].astype(F32).reshape(pc * c_loc, 128)
        if i + 2 < t_num:
            t_copy(i + 2).start()
        phase, row = divmod(i * pc, ph_rows)
        for c in range(c_loc):
            for j in range(0, v, 128):
                tt[phase, c, pl.ds(row, pc), pl.ds(j, 128)] = tf[j // 128, pl.ds(c, pc, stride=c_loc), :].astype(BF16)

    def compute(phase, q):
        def step(g, _):
            first = pl.multiple_of(g * group, group)
            t = tt[phase, pl.ds(first, group)].reshape(group * ph_rows, v)
            for a in range(A_WIN):
                x = jnp.dot(t, wa[q, a], preferred_element_type=F32).astype(BF16)
                for j in range(group):
                    xbuf[pl.ds(a * ph_rows, ph_rows), pl.ds(j * lc, lc)] = x[j * ph_rows : (j + 1) * ph_rows]
            block = bv[pl.ds(first, group), pl.ds(q * lc, lc), :].reshape(group * lc, v)
            acc[...] += jnp.dot(xbuf[...], block, preferred_element_type=F32)
            return 0

        lax.fori_loop(0, c_loc // group, step, 0)

    def a_copy(phase):
        return remote(acct.at[phase, 1 - core], recv_a.at[phase], a_send.at[phase], a_recv.at[phase], sib)

    def b_copy(phase, i):
        to = lax.rem(chip + i, k_num)
        return remote(summed.at[phase, to], recv_b.at[phase, i - 1], b_send.at[phase, i], b_recv.at[phase, i], to * 2 + core)

    def scatter_pair(phase):
        turned = jnp.transpose(acc[...])
        for j in range(n):
            acct[phase, j % 2, j // 2] = turned[j * vb : (j + 1) * vb]
        a_copy(phase).start()

    def scatter_chips(phase):
        a_copy(phase).wait_recv()
        summed[phase] = acct[phase, core] + recv_a[phase]
        for i in range(1, k_num):
            b_copy(phase, i).start()

    def scatter_end(phase):
        total = summed[phase, chip]
        for i in range(1, k_num):
            b_copy(phase, i).wait_recv()
            total = total + recv_b[phase, i - 1]
        out[phase] = total

    for q in range(q_num):
        extract(q)
    for i in range(t_num):
        turn(i)
    forward(0)
    for phase in range(PHASES):
        acc[...] = jnp.zeros_like(acc)
        for q in range(q_num):
            if phase == 0:
                finish(q)
                if q + 1 < q_num:
                    forward(q + 1)
                rest_copy(q).wait()
            compute(phase, q)
            if phase > 0 and q == 0:
                scatter_chips(phase - 1)
        scatter_pair(phase)
    scatter_chips(PHASES - 1)
    for phase in range(PHASES):
        scatter_end(phase)

    for q in range(q_num):
        for i in range(k_num):
            gather_copy(q, i).wait_send()
        for i in range(1, k_num):
            forward_copy(q, i).wait_send()
    for phase in range(PHASES):
        a_copy(phase).wait_send()
        for i in range(1, k_num):
            b_copy(phase, i).wait_send()


def shards(n, cholesky, amplitudes):
    c_loc, nchol, v = cholesky.shape
    p_size = amplitudes.shape[0]
    lc = min(256, nchol)
    q_num = nchol // lc
    k_num = n // 2
    group = min(4, c_loc)
    pc = min(32, p_size // PHASES)
    ph_rows = p_size // PHASES
    vb = v // n
    rows = A_WIN * ph_rows
    dma = pltpu.SemaphoreType.DMA
    flops = 4 * A_WIN * p_size * c_loc * nchol * v
    res = pl.pallas_call(
        functools.partial(kernel, n, lc, group, pc),
        out_shape=jax.ShapeDtypeStruct((PHASES, vb, rows), F32),
        in_specs=[pl.BlockSpec(memory_space=pl.ANY)] * 2,
        out_specs=pl.BlockSpec(memory_space=pltpu.VMEM),
        scratch_shapes=[
            pltpu.VMEM((c_loc, nchol, v), BF16),
            pltpu.VMEM((PHASES, c_loc, ph_rows, v), BF16),
            pltpu.VMEM((2, pc, c_loc, v), BF16),
            pltpu.VMEM((v // 128, pc * c_loc, 128), F32),
            pltpu.VMEM((c_loc, 128, 128), BF16),
            pltpu.VMEM((q_num, n, A_WIN * c_loc, lc), BF16),
            pltpu.VMEM((q_num, A_WIN, v, lc), BF16),
            pltpu.VMEM((rows, group * lc), BF16),
            pltpu.VMEM((rows, v), F32),
            pltpu.VMEM((PHASES, 2, k_num, vb, rows), F32),
            pltpu.VMEM((PHASES, k_num, vb, rows), F32),
            pltpu.VMEM((PHASES, k_num, vb, rows), F32),
            pltpu.VMEM((PHASES, k_num - 1, vb, rows), F32),
            dma((q_num,)),
            dma((q_num,)),
            dma((2,)),
            dma((q_num, k_num)),
            dma((q_num, k_num)),
            dma((q_num, k_num)),
            dma((q_num, k_num)),
            dma((PHASES,)),
            dma((PHASES,)),
            dma((PHASES, k_num)),
            dma((PHASES, k_num)),
        ],
        compiler_params=pltpu.CompilerParams(
            collective_id=0, has_side_effects=True, vmem_limit_bytes=62 * 1024 * 1024),
        cost_estimate=pl.CostEstimate(flops=flops, bytes_accessed=2 * (cholesky.size + amplitudes.size), transcendentals=0),
    )(cholesky, amplitudes)
    res = res.reshape(PHASES, vb, A_WIN, ph_rows)
    return jnp.transpose(res, (0, 3, 2, 1)).reshape(p_size, A_WIN, vb)


def solution(mesh):
    in_specs = (P(("ga", "col"), None, None), P("ga", "col", None))
    out_specs = P("ga", None, "col")
    body = functools.partial(shards, mesh.shape["col"])
    return jax.shard_map(body, mesh=mesh, in_specs=in_specs, out_specs=out_specs, check_vma=False)
```

```python
import functools

import jax
import jax.numpy as jnp
from jax import lax
from jax.experimental import pallas as pl
from jax.experimental.pallas import tpu as pltpu
from jax.sharding import PartitionSpec as P

A_WIN = 2
PHASES = 2
F32 = jnp.float32
BF16 = jnp.bfloat16
MESH = pl.DeviceIdType.MESH


def kernel(n, lc, group, pc, chol, amps, out, bv, tt, traw, tf, sel, w, wa, xbuf, acc, acct,
           recv_a, summed, recv_b, lane_sem, rest_sem, t_sem, g_send, g_recv, f_send, f_recv,
           a_send, a_recv, b_send, b_recv):
    c_loc, nchol, v = chol.shape
    p_size = amps.shape[0]
    q_num = nchol // lc
    k_num = n // 2
    vb = v // n
    ph_rows = p_size // PHASES
    me = lax.axis_index("col")
    chip = me // 2
    core = lax.rem(me, 2)
    sib = chip * 2 + 1 - core

    def peer_at(i):
        return lax.rem(chip + i, k_num) * 2 + core

    def source_at(i):
        return lax.rem(chip - i + k_num, k_num) * 2 + core

    def lane_copy(q):
        rows = pl.ds(pl.multiple_of(q * lc, lc), lc)
        return pltpu.make_async_copy(chol.at[:, rows, pl.ds(0, 128)], bv.at[:, rows, pl.ds(0, 128)], lane_sem.at[q])

    def rest_copy(q):
        rows = pl.ds(pl.multiple_of(q * lc, lc), lc)
        return pltpu.make_async_copy(chol.at[:, rows, pl.ds(128, v - 128)], bv.at[:, rows, pl.ds(128, v - 128)], rest_sem.at[q])

    t_num = p_size // pc

    def t_copy(i):
        return pltpu.make_async_copy(amps.at[pl.ds(i * pc, pc)], traw.at[lax.rem(i, 2)], t_sem.at[lax.rem(i, 2)])

    for q in range(q_num):
        lane_copy(q).start()
    t_copy(0).start()
    t_copy(1).start()
    for q in range(q_num):
        rest_copy(q).start()

    barrier = pltpu.get_barrier_semaphore()
    pl.semaphore_signal(barrier, inc=1, device_id={"col": sib}, device_id_type=MESH)
    for i in range(1, k_num):
        pl.semaphore_signal(barrier, inc=1, device_id={"col": peer_at(i)}, device_id_type=MESH)

    lane = lax.broadcasted_iota(jnp.int32, (128, 128), 0)
    column = lax.broadcasted_iota(jnp.int32, (128, 128), 1)

    def make_sel(c, _):
        sel[c] = jnp.where((lane < A_WIN) & (column == lane * c_loc + c), 1.0, 0.0).astype(BF16)
        return 0

    lax.fori_loop(0, c_loc, make_sel, 0)
    pl.semaphore_wait(barrier, k_num)

    def remote(src, dst, send, recv, to):
        return pltpu.make_async_remote_copy(
            src_ref=src, dst_ref=dst, send_sem=send, recv_sem=recv, device_id={"col": to}, device_id_type=MESH)

    def gather_copy(q, i):
        to = sib if i == 0 else peer_at(i)
        return remote(w.at[q, me], w.at[q, me], g_send.at[q, i], g_recv.at[q, i], to)

    def forward_copy(q, i):
        block = w.at[q, source_at(i)]
        return remote(block, block, f_send.at[q, i], f_recv.at[q, i], sib)

    def extract(q):
        lane_copy(q).wait()

        def step(c, z):
            return z + jnp.dot(bv[c, pl.ds(pl.multiple_of(q * lc, lc), lc), pl.ds(0, 128)], sel[c], preferred_element_type=F32)

        z = lax.fori_loop(0, c_loc, step, jnp.zeros((lc, 128), F32), unroll=4)
        w[q, me] = jnp.transpose(z)[: A_WIN * c_loc].astype(BF16)
        for i in range(k_num):
            gather_copy(q, i).start()

    def forward(q):
        for i in range(1, k_num):
            gather_copy(q, i).wait_recv()
            forward_copy(q, i).start()

    def finish(q):
        gather_copy(q, 0).wait_recv()
        for i in range(1, k_num):
            forward_copy(q, i).wait_recv()
        whole = w[q].astype(F32)
        for a in range(A_WIN):
            wa[q, a] = whole[:, a * c_loc : (a + 1) * c_loc, :].reshape(v, lc).astype(BF16)

    def turn(i):
        t_copy(i).wait()
        for j in range(0, v, 128):
            tf[j // 128] = traw[lax.rem(i, 2), :, :, pl.ds(j, 128)].astype(F32).reshape(pc * c_loc, 128)

        @pl.when(i + 2 < t_num)
        def _():
            t_copy(i + 2).start()

        phase = i * pc // ph_rows
        row = pl.multiple_of(lax.rem(i * pc, ph_rows), pc)
        for c in range(c_loc):
            for j in range(0, v, 128):
                tt[phase, c, pl.ds(row, pc), pl.ds(j, 128)] = tf[j // 128, pl.ds(c, pc, stride=c_loc), :].astype(BF16)

    def compute(phase, q):
        def step(g, _):
            first = pl.multiple_of(g * group, group)
            t = tt[phase, pl.ds(first, group)].reshape(group * ph_rows, v)
            for a in range(A_WIN):
                x = jnp.dot(t, wa[q, a], preferred_element_type=F32).astype(BF16)
                for j in range(group):
                    xbuf[pl.ds(a * ph_rows, ph_rows), pl.ds(j * lc, lc)] = x[j * ph_rows : (j + 1) * ph_rows]
            block = bv[pl.ds(first, group), pl.ds(pl.multiple_of(q * lc, lc), lc), :].reshape(group * lc, v)
            acc[...] += jnp.dot(xbuf[...], block, preferred_element_type=F32)
            return 0

        lax.fori_loop(0, c_loc // group, step, 0, unroll=2)

    def a_copy(phase):
        return remote(acct.at[phase, 1 - core], recv_a.at[phase], a_send.at[phase], a_recv.at[phase], sib)

    def b_copy(phase, i):
        to = lax.rem(chip + i, k_num)
        return remote(summed.at[phase, to], recv_b.at[phase, i - 1], b_send.at[phase, i], b_recv.at[phase, i], to * 2 + core)

    def scatter_pair(phase):
        turned = jnp.transpose(acc[...])
        for j in range(n):
            acct[phase, j % 2, j // 2] = turned[j * vb : (j + 1) * vb]
        a_copy(phase).start()

    def scatter_chips(phase):
        a_copy(phase).wait_recv()
        summed[phase] = acct[phase, core] + recv_a[phase]
        for i in range(1, k_num):
            b_copy(phase, i).start()

    def scatter_end(phase):
        total = summed[phase, chip]
        for i in range(1, k_num):
            b_copy(phase, i).wait_recv()
            total = total + recv_b[phase, i - 1]
        out[phase] = total

    def loop(count, body):
        def step(i, _):
            body(i)
            return 0

        lax.fori_loop(0, count, step, 0)

    loop(q_num, extract)
    loop(t_num, turn)
    forward(0)

    def chunk(i):
        phase, q = i // q_num, lax.rem(i, q_num)

        @pl.when(q == 0)
        def _():
            acc[...] = jnp.zeros_like(acc)

        @pl.when(phase == 0)
        def _():
            finish(q)

            @pl.when(q + 1 < q_num)
            def _():
                forward(q + 1)

            rest_copy(q).wait()

        compute(phase, q)

        @pl.when((phase > 0) & (q == 0))
        def _():
            scatter_chips(phase - 1)

        @pl.when(q == q_num - 1)
        def _():
            scatter_pair(phase)

    loop(PHASES * q_num, chunk)
    scatter_chips(PHASES - 1)
    for phase in range(PHASES):
        scatter_end(phase)

    for q in range(q_num):
        for i in range(k_num):
            gather_copy(q, i).wait_send()
        for i in range(1, k_num):
            forward_copy(q, i).wait_send()
    for phase in range(PHASES):
        a_copy(phase).wait_send()
        for i in range(1, k_num):
            b_copy(phase, i).wait_send()


def shards(n, cholesky, amplitudes):
    c_loc, nchol, v = cholesky.shape
    p_size = amplitudes.shape[0]
    lc = min(256, nchol)
    q_num = nchol // lc
    k_num = n // 2
    group = min(4, c_loc)
    pc = min(32, p_size // PHASES)
    ph_rows = p_size // PHASES
    vb = v // n
    rows = A_WIN * ph_rows
    dma = pltpu.SemaphoreType.DMA
    flops = 4 * A_WIN * p_size * c_loc * nchol * v
    res = pl.pallas_call(
        functools.partial(kernel, n, lc, group, pc),
        out_shape=jax.ShapeDtypeStruct((PHASES, vb, rows), F32),
        in_specs=[pl.BlockSpec(memory_space=pl.ANY)] * 2,
        out_specs=pl.BlockSpec(memory_space=pltpu.VMEM),
        scratch_shapes=[
            pltpu.VMEM((c_loc, nchol, v), BF16),
            pltpu.VMEM((PHASES, c_loc, ph_rows, v), BF16),
            pltpu.VMEM((2, pc, c_loc, v), BF16),
            pltpu.VMEM((v // 128, pc * c_loc, 128), F32),
            pltpu.VMEM((c_loc, 128, 128), BF16),
            pltpu.VMEM((q_num, n, A_WIN * c_loc, lc), BF16),
            pltpu.VMEM((q_num, A_WIN, v, lc), BF16),
            pltpu.VMEM((rows, group * lc), BF16),
            pltpu.VMEM((rows, v), F32),
            pltpu.VMEM((PHASES, 2, k_num, vb, rows), F32),
            pltpu.VMEM((PHASES, k_num, vb, rows), F32),
            pltpu.VMEM((PHASES, k_num, vb, rows), F32),
            pltpu.VMEM((PHASES, k_num - 1, vb, rows), F32),
            dma((q_num,)),
            dma((q_num,)),
            dma((2,)),
            dma((q_num, k_num)),
            dma((q_num, k_num)),
            dma((q_num, k_num)),
            dma((q_num, k_num)),
            dma((PHASES,)),
            dma((PHASES,)),
            dma((PHASES, k_num)),
            dma((PHASES, k_num)),
        ],
        compiler_params=pltpu.CompilerParams(
            collective_id=0, has_side_effects=True, vmem_limit_bytes=62 * 1024 * 1024),
        cost_estimate=pl.CostEstimate(flops=flops, bytes_accessed=2 * (cholesky.size + amplitudes.size), transcendentals=0),
    )(cholesky, amplitudes)
    res = res.reshape(PHASES, vb, A_WIN, ph_rows)
    return jnp.transpose(res, (0, 3, 2, 1)).reshape(p_size, A_WIN, vb)


def solution(mesh):
    in_specs = (P(("ga", "col"), None, None), P("ga", "col", None))
    out_specs = P("ga", None, "col")
    body = functools.partial(shards, mesh.shape["col"])
    return jax.shard_map(body, mesh=mesh, in_specs=in_specs, out_specs=out_specs, check_vma=False)
```
